32 devices in a mesh: seq: 8 (over z, x), head: 4 (over y, core).
Axes of the slice: x: 2, y: 2, z: 4, core: 2. Of those that a mesh axis runs over, the one named last changes fastest.
Arguments:
- queries: bfloat16 [8192, 4096], P(('seq', 'head')), may hold values from -16 to 16
- keys: bfloat16 [8192, 4096], P(('seq', 'head')), may hold values from -16 to 16
- values: bfloat16 [8192, 4096], P(('seq', 'head')), may hold values from -12 to 12
Outputs:
- attended: bfloat16 [8192, 4096], P(('seq', 'head'))
The draws below stay inside these ranges and needn't reach their ends.
All inputs are finite; a program needn't handle non-finite values.
Results may differ from the reference program's by a relative error of at most 0.0041.
Values may be sent and summed in bfloat16 or wider, within the bound.
A program may use at most 128 MiB of HBM per device.

```python
import math
import jax
import jax.numpy as jnp
from jax import lax

HEADS = 32
HD = 128
D = 4096
BLOCK = 128
TOKENS = 8192


def draw_queries(key, part):
    key = jax.random.fold_in(key, 1)
    noise = jnp.clip(jax.random.normal(jax.random.fold_in(key, 2), (TOKENS, D), jnp.float32), -4.0, 4.0)
    return (1.8 * noise).astype(jnp.bfloat16)


def draw_keys(key, part):
    key = jax.random.fold_in(key, 2)
    noise = jnp.clip(jax.random.normal(jax.random.fold_in(key, 3), (TOKENS, D), jnp.float32), -4.0, 4.0)
    return (1.8 * noise).astype(jnp.bfloat16)


def draw_values(key, part):
    key = jax.random.fold_in(key, 3)
    region = jnp.arange(TOKENS) // max(1, TOKENS // 16)
    offsets = jnp.clip(jax.random.normal(jax.random.fold_in(key, 1), (16, D), jnp.float32), -4.0, 4.0)
    noise = jnp.clip(jax.random.normal(jax.random.fold_in(key, 2), (TOKENS, D), jnp.float32), -5.0, 5.0)
    return (0.6 * noise + 0.8 * offsets[region]).astype(jnp.bfloat16)


def setup_inputs(seed: int = 0) -> dict:
    streams_of = jax.random.split(jax.random.key(seed), 4)
    queries = draw_queries(jax.random.fold_in(streams_of[3], 71), 0)
    keys = draw_keys(jax.random.fold_in(streams_of[3], 71), 0)
    values = draw_values(jax.random.fold_in(streams_of[3], 71), 0)
    return dict(queries=queries, keys=keys, values=values)


def halve(field):
    rows = field.shape[0]
    paired = field.astype(jnp.float32).reshape(rows // 2, 2, field.shape[1])
    return ((paired[:, 0] + paired[:, 1]) * 0.5).astype(jnp.bfloat16)

def merge_level(state, level):
    best, numerator, denominator = state
    level_top, level_numerator, level_denominator = level
    joint = jnp.maximum(best, level_top)
    old_weight = jnp.exp(best - joint)
    new_weight = jnp.exp(level_top - joint)
    return (joint, numerator * old_weight[:, None] + level_numerator * new_weight[:, None], denominator * old_weight + level_denominator * new_weight)

def one_head(head_inputs):
    query, key_rows, value_rows = head_inputs
    length = query.shape[0]
    scale = 1.0 / math.sqrt(HD)
    blocks = length // BLOCK
    query_wide = query.astype(jnp.float32)
    leaf_queries = query_wide.reshape(blocks, BLOCK, HD)
    leaf_keys = key_rows.astype(jnp.float32).reshape(blocks, BLOCK, HD)
    leaf_values = value_rows.astype(jnp.float32).reshape(blocks, BLOCK, HD)
    scores = jnp.einsum('nid,njd->nij', leaf_queries, leaf_keys) * scale
    causal = jnp.arange(BLOCK)[:, None] >= jnp.arange(BLOCK)[None, :]
    top = lax.optimization_barrier(jnp.max(jnp.where(causal, scores, -jnp.inf), axis=-1))
    weights = jnp.where(causal, jnp.exp(scores - top[..., None]), 0.0)
    rounded = weights.astype(jnp.bfloat16).astype(jnp.float32)
    numerator = jnp.einsum('nij,njd->nid', rounded, leaf_values)
    state = (top.reshape(length), numerator.reshape(length, HD), lax.optimization_barrier(jnp.sum(weights, axis=-1)).reshape(length))
    levels = (length // BLOCK).bit_length() - 1
    coarse_keys, coarse_values = (key_rows, value_rows)
    for level in range(1, levels + 1):
        span = BLOCK * 2 ** (level - 1)
        pairs = length // (2 * span)
        upper_queries = query_wide.reshape(pairs, 2, span, HD)[:, 1]
        lower_keys = coarse_keys.astype(jnp.float32).reshape(pairs, 2, BLOCK, HD)[:, 0]
        lower_values = coarse_values.astype(jnp.float32).reshape(pairs, 2, BLOCK, HD)[:, 0]
        scores = jnp.einsum('npd,nbd->npb', upper_queries, lower_keys) * scale + (level - 1) * math.log(2.0)
        top = lax.optimization_barrier(jnp.max(scores, axis=-1))
        weights = jnp.exp(scores - top[..., None])
        rounded = weights.astype(jnp.bfloat16).astype(jnp.float32)
        numerator = jnp.einsum('npb,nbd->npd', rounded, lower_values)
        denominator = lax.optimization_barrier(jnp.sum(weights, axis=-1))
        top_full = jnp.stack([jnp.full_like(top, -jnp.inf), top], axis=1).reshape(length)
        numerator_full = jnp.stack([jnp.zeros_like(numerator), numerator], axis=1).reshape(length, HD)
        denominator_full = jnp.stack([jnp.zeros_like(denominator), denominator], axis=1).reshape(length)
        state = merge_level(state, (top_full, numerator_full, denominator_full))
        if level < levels:
            coarse_keys = halve(coarse_keys)
            coarse_values = halve(coarse_values)
    best, numerator, denominator = state
    return (numerator / denominator[:, None]).astype(jnp.bfloat16)

def split_heads(array):
    return array.reshape(TOKENS, HEADS, HD).transpose(1, 0, 2)

def reference(queries, keys, values):
    results = lax.map(one_head, (split_heads(queries), split_heads(keys), split_heads(values)))
    return results.transpose(1, 0, 2).reshape(TOKENS, HEADS * HD)
```

```python
import functools
import math

import jax
import jax.numpy as jnp
from jax import lax
from jax.experimental import pallas as pl
from jax.experimental.pallas import tpu as pltpu
from jax.sharding import PartitionSpec as P

HD = 128
BLOCK = 128


def swapped(x, axis, distance):
    return lax.ppermute(x, axis, [(i, i ^ 1 << distance) for i in range(lax.axis_size(axis))])


def halve(field):
    rows = field.shape[0]
    paired = field.astype(jnp.float32).reshape((rows // 2, 2) + field.shape[1:])
    return ((paired[:, 0] + paired[:, 1]) * 0.5).astype(jnp.bfloat16)


def merge_level(state, level):
    best, numerator, denominator = state
    level_top, level_numerator, level_denominator = level
    joint = jnp.maximum(best, level_top)
    old_weight = jnp.exp(best - joint)
    new_weight = jnp.exp(level_top - joint)
    return (
        joint,
        numerator * old_weight[:, :, None] + level_numerator * new_weight[:, :, None],
        denominator * old_weight + level_denominator * new_weight,
    )


def leaf_level(query, keys_local, values_local, scale):
    length, heads, width = query.shape
    blocks = length // BLOCK
    shaped = (blocks, BLOCK, heads, width)
    scores = (
        jnp.einsum(
            "nigd,njgd->ngij",
            query.reshape(shaped),
            keys_local.reshape(shaped),
            preferred_element_type=jnp.float32,
        )
        * scale
    )
    causal = jnp.arange(BLOCK)[:, None] >= jnp.arange(BLOCK)[None, :]
    top = jnp.max(jnp.where(causal, scores, -jnp.inf), axis=-1)
    weights = jnp.where(causal, jnp.exp(scores - top[..., None]), 0.0)
    numerator = jnp.einsum(
        "ngij,njgd->nigd",
        weights.astype(jnp.bfloat16),
        values_local.reshape(shaped),
        preferred_element_type=jnp.float32,
    )
    denominator = jnp.sum(weights, axis=-1)
    top = top.transpose(0, 2, 1).reshape(length, heads)
    denominator = denominator.transpose(0, 2, 1).reshape(length, heads)
    return (top, numerator.reshape(length, heads, width), denominator)


def pair_level(query, coarse_keys, coarse_values, level, scale):
    length, heads, width = query.shape
    span = BLOCK * 2 ** (level - 1)
    pairs = length // (2 * span)
    upper_queries = query.reshape(pairs, 2, span, heads, width)[:, 1]
    lower_keys = coarse_keys.reshape(pairs, 2, BLOCK, heads, width)[:, 0]
    lower_values = coarse_values.reshape(pairs, 2, BLOCK, heads, width)[:, 0]
    scores = jnp.einsum(
        "npgd,nbgd->npgb", upper_queries, lower_keys, preferred_element_type=jnp.float32
    ) * scale + (level - 1) * math.log(2.0)
    top = jnp.max(scores, axis=-1)
    weights = jnp.exp(scores - top[..., None])
    numerator = jnp.einsum(
        "npgb,nbgd->npgd",
        weights.astype(jnp.bfloat16),
        lower_values,
        preferred_element_type=jnp.float32,
    )
    denominator = jnp.sum(weights, axis=-1)
    top_full = jnp.stack([jnp.full_like(top, -jnp.inf), top], axis=1).reshape(length, heads)
    numerator_full = jnp.stack([jnp.zeros_like(numerator), numerator], axis=1).reshape(
        length, heads, width
    )
    denominator_full = jnp.stack([jnp.zeros_like(denominator), denominator], axis=1).reshape(
        length, heads
    )
    return (top_full, numerator_full, denominator_full)


def far_level(query, tile_keys, tile_values, level, scale, upper):
    length, heads, width = query.shape

    def active():
        scores = jnp.einsum(
            "sgd,bgd->sgb", query, tile_keys, preferred_element_type=jnp.float32
        ) * scale + (level - 1) * math.log(2.0)
        top = jnp.max(scores, axis=-1)
        weights = jnp.exp(scores - top[..., None])
        numerator = jnp.einsum(
            "sgb,bgd->sgd",
            weights.astype(jnp.bfloat16),
            tile_values,
            preferred_element_type=jnp.float32,
        )
        return (top, numerator, jnp.sum(weights, axis=-1))

    def quiet():
        return (
            jnp.full((length, heads), -jnp.inf, jnp.float32),
            jnp.zeros((length, heads, width), jnp.float32),
            jnp.zeros((length, heads), jnp.float32),
        )

    return lax.cond(upper == 1, active, quiet)


def local_part(query, keys_local, values_local, scale):
    state = leaf_level(query, keys_local, values_local, scale)
    depth = (query.shape[0] // BLOCK).bit_length() - 1
    coarse_keys, coarse_values = (keys_local, values_local)
    state = merge_level(state, pair_level(query, coarse_keys, coarse_values, 1, scale))
    coarse_keys = halve(coarse_keys)
    coarse_values = halve(coarse_values)
    return (state, coarse_keys, coarse_values, depth + 1)


def doubling(query, state, tile_keys, tile_values, first, count, position, trade, scale):
    for step in range(count):
        other_keys, other_values = trade(tile_keys, tile_values, step)
        upper = position // 2**step % 2
        state = merge_level(
            state, far_level(query, other_keys, other_values, first + step, scale, upper)
        )
        if step + 1 < count:
            high = upper == 1
            low_keys = jnp.where(high, other_keys, tile_keys)
            high_keys = jnp.where(high, tile_keys, other_keys)
            low_values = jnp.where(high, other_values, tile_values)
            high_values = jnp.where(high, tile_values, other_values)
            tile_keys = halve(jnp.concatenate([low_keys, high_keys], axis=0))
            tile_values = halve(jnp.concatenate([low_values, high_values], axis=0))
    return state


def finish(state):
    best, numerator, denominator = state
    length, heads, width = numerator.shape
    return (numerator / denominator[:, :, None]).astype(jnp.bfloat16).reshape(length, heads * width)


def shards(queries, keys, values):
    scale = 1.0 / math.sqrt(HD)
    length, width = queries.shape
    cube_shape = (length, width // HD, HD)
    query = queries.reshape(cube_shape)
    state, tile_keys, tile_values, first = local_part(
        query, keys.reshape(cube_shape), values.reshape(cube_shape), scale
    )
    position = lax.axis_index(("seq", "head"))
    count = lax.axis_size(("seq", "head")).bit_length() - 1

    def trade_all(send_keys, send_values, bit):
        return swapped((send_keys, send_values), ("seq", "head"), bit)

    state = doubling(query, state, tile_keys, tile_values, first, count, position, trade_all, scale)
    return finish(state)


LEVELS = 5
ORDER = {0: (), 1: (0,), 2: (1, 0), 3: (1, 2, 0), 4: (1, 2, 3, 0)}
COPIES = [(s, i) for s in range(LEVELS) for i in range(-1, s)]
MESH = pl.DeviceIdType.MESH
BASE2 = math.log2(math.e) / math.sqrt(HD)


def halving(rows):
    out = lax.broadcasted_iota(jnp.int32, (rows // 2, rows), 0)
    into = lax.broadcasted_iota(jnp.int32, (rows // 2, rows), 1)
    return jnp.where(into // 2 == out, 0.5, 0.0).astype(jnp.bfloat16)


def scores_of(keys, query):
    return lax.dot_general(keys, query, (((1,), (1,)), ((), ())), preferred_element_type=jnp.float32)


def weighted(values, weights):
    return lax.dot_general(
        values, weights.astype(jnp.bfloat16), (((0,), (0,)), ((), ())), preferred_element_type=jnp.float32
    )


def softened(scores):
    top = jnp.max(scores, axis=0, keepdims=True)
    weights = jnp.exp2((scores - top) * BASE2)
    return top * BASE2, weights, jnp.sum(weights, axis=0, keepdims=True)


def merged(old, new):
    joint = jnp.maximum(old[0], new[0])
    old_weight = jnp.exp2(old[0] - joint)
    new_weight = jnp.exp2(new[0] - joint)
    return (
        joint,
        old[1] * old_weight + new[1] * new_weight,
        old[2] * old_weight + new[2] * new_weight,
    )


def kernel(head_bits, q_ref, k_ref, v_ref, o_ref, *scratch):
    pyramid = scratch[:LEVELS]
    tiles = scratch[LEVELS : 2 * LEVELS]
    numerators, tops, denominators, send_sems, recv_sems = scratch[2 * LEVELS :]
    width = q_ref.shape[1]
    heads = width // HD
    seq, head = lax.axis_index("seq"), lax.axis_index("head")

    def bit(b):
        return head // 2**b % 2 if b < head_bits else seq // 2 ** (b - head_bits) % 2

    def partner(b):
        step = 1 - 2 * bit(b)
        if b < head_bits:
            return (seq, head + step * 2**b)
        return (seq + step * 2 ** (b - head_bits), head)

    def slot(s):
        where = 0
        for i, b in enumerate(ORDER[s]):
            where = where + bit(b) * 2**i
        return where

    def copy(s, i):
        n = COPIES.index((s, i))
        if i < 0:
            source, target, b = pyramid[s], tiles[s].at[slot(s)], s
        else:
            block = pl.ds(slot(s) // 2**i * 2**i, 2**i)
            source = target = tiles[s].at[block]
            b = ORDER[s][i]
        return pltpu.make_async_remote_copy(
            src_ref=source, dst_ref=target, send_sem=send_sems.at[n], recv_sem=recv_sems.at[n],
            device_id=partner(b), device_id_type=MESH,
        )

    def landed(s, i):
        @pl.when(bit(s) == 1)
        def _():
            copy(s, i).wait_recv()
            if i + 1 < s:
                copy(s, i + 1).start()

    barrier = pltpu.get_barrier_semaphore()
    for b in range(LEVELS):
        pl.semaphore_signal(barrier, inc=1, device_id=partner(b), device_id_type=MESH)

    chunk = 512

    @pl.loop(0, width // chunk)
    def _(c):
        columns = pl.ds(pl.multiple_of(c * chunk, chunk), chunk)
        keys, values = k_ref[:, columns], v_ref[:, columns]
        for s in range(LEVELS):
            rows = BLOCK // 2**s
            mean = halving(2 * rows)
            keys = jnp.dot(mean, keys, preferred_element_type=jnp.float32)
            values = jnp.dot(mean, values, preferred_element_type=jnp.float32)
            pyramid[s][:, columns] = jnp.concatenate([keys, values], axis=0).astype(jnp.bfloat16)
            keys, values = keys.astype(jnp.bfloat16), values.astype(jnp.bfloat16)

    pl.semaphore_wait(barrier, LEVELS)
    for s in (1, 2, 3, 4, 0):
        @pl.when(bit(s) == 0)
        def _():
            copy(s, -1).start()

    def columns_of(h):
        return pl.ds(pl.multiple_of(h * HD, HD), HD)

    def store(h, state):
        tops[h] = state[0]
        numerators[h] = state[1]
        denominators[h] = state[2]

    def local(h):
        columns = columns_of(h)
        key = lax.broadcasted_iota(jnp.int32, (BLOCK, BLOCK), 0)
        token = lax.broadcasted_iota(jnp.int32, (BLOCK, BLOCK), 1)
        causal = key <= token
        low, high = pl.ds(0, BLOCK), pl.ds(BLOCK, BLOCK)

        def level(block, rows, mask):
            scores = scores_of(k_ref[rows, columns], q_ref[block, columns])
            if mask:
                scores = jnp.where(causal, scores, -jnp.inf)
            top, weights, total = softened(scores)
            return top, weighted(v_ref[rows, columns], weights), total

        first = level(low, low, True)
        second = merged(level(high, high, True), level(high, low, False))
        store(h, [jnp.concatenate(two, axis=1) for two in zip(first, second)])

    def far(s):
        rows = BLOCK // 2**s

        def of_head(h):
            columns = columns_of(h)
            if rows >= 16:
                keys = tiles[s][:, :rows, columns].reshape(BLOCK, HD)
                values = tiles[s][:, rows:, columns].reshape(BLOCK, HD)
            else:
                both = tiles[s][:, :, columns].astype(jnp.float32)
                keys = both[:, :rows].reshape(BLOCK, HD).astype(jnp.bfloat16)
                values = both[:, rows:].reshape(BLOCK, HD).astype(jnp.bfloat16)
            top, weights, total = softened(scores_of(keys, q_ref[:, columns]))
            level = (top + (s + 1.0), weighted(values, weights), total)
            store(h, merged((tops[h], numerators[h], denominators[h]), level))

        @pl.when(bit(s) == 1)
        def _():
            each(of_head)

    def each(of_head):
        @pl.loop(0, heads // UNROLL)
        def _(g):
            for u in range(UNROLL):
                of_head(g * UNROLL + u)

    def final(h):
        result = numerators[h] / denominators[h]
        o_ref[:, columns_of(h)] = result.T.astype(o_ref.dtype)

    each(local)
    landed(3, -1)
    landed(4, -1)
    landed(0, -1)
    far(0)
    landed(2, -1)
    landed(4, 0)
    landed(3, 0)
    landed(4, 1)
    landed(1, -1)
    landed(3, 1)
    landed(1, 0)
    far(1)
    landed(2, 0)
    landed(4, 2)
    landed(3, 2)
    far(3)
    landed(2, 1)
    far(2)
    landed(4, 3)
    far(4)
    each(final)
    for s, i in COPIES:
        @pl.when(bit(s) == (0 if i < 0 else 1))
        def _():
            copy(s, i).wait_send()


UNROLL = 2


def fused(head_bits, queries, keys, values):
    length, width = queries.shape
    heads = width // HD
    pieces = [(2 * BLOCK // 2**s, width) for s in range(LEVELS)]
    scratch = [pltpu.VMEM(p, jnp.bfloat16) for p in pieces]
    scratch += [pltpu.VMEM((2**s,) + p, jnp.bfloat16) for s, p in enumerate(pieces)]
    scratch += [
        pltpu.VMEM((heads, HD, length), jnp.float32),
        pltpu.VMEM((heads, 1, length), jnp.float32),
        pltpu.VMEM((heads, 1, length), jnp.float32),
        pltpu.SemaphoreType.DMA((len(COPIES),)),
        pltpu.SemaphoreType.DMA((len(COPIES),)),
    ]
    return pl.pallas_call(
        functools.partial(kernel, head_bits),
        out_shape=jax.ShapeDtypeStruct((length, width), jnp.bfloat16),
        in_specs=[pl.BlockSpec(memory_space=pltpu.VMEM)] * 3,
        out_specs=pl.BlockSpec(memory_space=pltpu.VMEM),
        scratch_shapes=scratch,
        compiler_params=pltpu.CompilerParams(
            collective_id=0, has_side_effects=True, vmem_limit_bytes=48 * 2**20
        ),
    )(queries, keys, values)


def solution(mesh):
    if mesh.size == 2**LEVELS:
        body = functools.partial(fused, mesh.shape["head"].bit_length() - 1)
    else:
        body = shards
    return jax.shard_map(
        body,
        mesh=mesh,
        in_specs=(P(("seq", "head"), None), P(("seq", "head"), None), P(("seq", "head"), None)),
        out_specs=P(("seq", "head"), None),
        check_vma=False,
    )
```

```python
import functools
import math

import jax
import jax.numpy as jnp
from jax import lax
from jax.experimental import pallas as pl
from jax.experimental.pallas import tpu as pltpu
from jax.sharding import PartitionSpec as P

HD = 128
BLOCK = 128


def swapped(x, axis, distance):
    return lax.ppermute(x, axis, [(i, i ^ 1 << distance) for i in range(lax.axis_size(axis))])


def halve(field):
    rows = field.shape[0]
    paired = field.astype(jnp.float32).reshape((rows // 2, 2) + field.shape[1:])
    return ((paired[:, 0] + paired[:, 1]) * 0.5).astype(jnp.bfloat16)


def merge_level(state, level):
    best, numerator, denominator = state
    level_top, level_numerator, level_denominator = level
    joint = jnp.maximum(best, level_top)
    old_weight = jnp.exp(best - joint)
    new_weight = jnp.exp(level_top - joint)
    return (
        joint,
        numerator * old_weight[:, :, None] + level_numerator * new_weight[:, :, None],
        denominator * old_weight + level_denominator * new_weight,
    )


def leaf_level(query, keys_local, values_local, scale):
    length, heads, width = query.shape
    blocks = length // BLOCK
    shaped = (blocks, BLOCK, heads, width)
    scores = (
        jnp.einsum(
            "nigd,njgd->ngij",
            query.reshape(shaped),
            keys_local.reshape(shaped),
            preferred_element_type=jnp.float32,
        )
        * scale
    )
    causal = jnp.arange(BLOCK)[:, None] >= jnp.arange(BLOCK)[None, :]
    top = jnp.max(jnp.where(causal, scores, -jnp.inf), axis=-1)
    weights = jnp.where(causal, jnp.exp(scores - top[..., None]), 0.0)
    numerator = jnp.einsum(
        "ngij,njgd->nigd",
        weights.astype(jnp.bfloat16),
        values_local.reshape(shaped),
        preferred_element_type=jnp.float32,
    )
    denominator = jnp.sum(weights, axis=-1)
    top = top.transpose(0, 2, 1).reshape(length, heads)
    denominator = denominator.transpose(0, 2, 1).reshape(length, heads)
    return (top, numerator.reshape(length, heads, width), denominator)


def pair_level(query, coarse_keys, coarse_values, level, scale):
    length, heads, width = query.shape
    span = BLOCK * 2 ** (level - 1)
    pairs = length // (2 * span)
    upper_queries = query.reshape(pairs, 2, span, heads, width)[:, 1]
    lower_keys = coarse_keys.reshape(pairs, 2, BLOCK, heads, width)[:, 0]
    lower_values = coarse_values.reshape(pairs, 2, BLOCK, heads, width)[:, 0]
    scores = jnp.einsum(
        "npgd,nbgd->npgb", upper_queries, lower_keys, preferred_element_type=jnp.float32
    ) * scale + (level - 1) * math.log(2.0)
    top = jnp.max(scores, axis=-1)
    weights = jnp.exp(scores - top[..., None])
    numerator = jnp.einsum(
        "npgb,nbgd->npgd",
        weights.astype(jnp.bfloat16),
        lower_values,
        preferred_element_type=jnp.float32,
    )
    denominator = jnp.sum(weights, axis=-1)
    top_full = jnp.stack([jnp.full_like(top, -jnp.inf), top], axis=1).reshape(length, heads)
    numerator_full = jnp.stack([jnp.zeros_like(numerator), numerator], axis=1).reshape(
        length, heads, width
    )
    denominator_full = jnp.stack([jnp.zeros_like(denominator), denominator], axis=1).reshape(
        length, heads
    )
    return (top_full, numerator_full, denominator_full)


def far_level(query, tile_keys, tile_values, level, scale, upper):
    length, heads, width = query.shape

    def active():
        scores = jnp.einsum(
            "sgd,bgd->sgb", query, tile_keys, preferred_element_type=jnp.float32
        ) * scale + (level - 1) * math.log(2.0)
        top = jnp.max(scores, axis=-1)
        weights = jnp.exp(scores - top[..., None])
        numerator = jnp.einsum(
            "sgb,bgd->sgd",
            weights.astype(jnp.bfloat16),
            tile_values,
            preferred_element_type=jnp.float32,
        )
        return (top, numerator, jnp.sum(weights, axis=-1))

    def quiet():
        return (
            jnp.full((length, heads), -jnp.inf, jnp.float32),
            jnp.zeros((length, heads, width), jnp.float32),
            jnp.zeros((length, heads), jnp.float32),
        )

    return lax.cond(upper == 1, active, quiet)


def local_part(query, keys_local, values_local, scale):
    state = leaf_level(query, keys_local, values_local, scale)
    depth = (query.shape[0] // BLOCK).bit_length() - 1
    coarse_keys, coarse_values = (keys_local, values_local)
    state = merge_level(state, pair_level(query, coarse_keys, coarse_values, 1, scale))
    coarse_keys = halve(coarse_keys)
    coarse_values = halve(coarse_values)
    return (state, coarse_keys, coarse_values, depth + 1)


def doubling(query, state, tile_keys, tile_values, first, count, position, trade, scale):
    for step in range(count):
        other_keys, other_values = trade(tile_keys, tile_values, step)
        upper = position // 2**step % 2
        state = merge_level(
            state, far_level(query, other_keys, other_values, first + step, scale, upper)
        )
        if step + 1 < count:
            high = upper == 1
            low_keys = jnp.where(high, other_keys, tile_keys)
            high_keys = jnp.where(high, tile_keys, other_keys)
            low_values = jnp.where(high, other_values, tile_values)
            high_values = jnp.where(high, tile_values, other_values)
            tile_keys = halve(jnp.concatenate([low_keys, high_keys], axis=0))
            tile_values = halve(jnp.concatenate([low_values, high_values], axis=0))
    return state


def finish(state):
    best, numerator, denominator = state
    length, heads, width = numerator.shape
    return (numerator / denominator[:, :, None]).astype(jnp.bfloat16).reshape(length, heads * width)


def shards(queries, keys, values):
    scale = 1.0 / math.sqrt(HD)
    length, width = queries.shape
    cube_shape = (length, width // HD, HD)
    query = queries.reshape(cube_shape)
    state, tile_keys, tile_values, first = local_part(
        query, keys.reshape(cube_shape), values.reshape(cube_shape), scale
    )
    position = lax.axis_index(("seq", "head"))
    count = lax.axis_size(("seq", "head")).bit_length() - 1

    def trade_all(send_keys, send_values, bit):
        return swapped((send_keys, send_values), ("seq", "head"), bit)

    state = doubling(query, state, tile_keys, tile_values, first, count, position, trade_all, scale)
    return finish(state)


LEVELS = 5
ORDER = {0: (), 1: (0,), 2: (1, 0), 3: (1, 2, 0), 4: (1, 2, 3, 0)}
PARTS = 2
COPIES = [(s, i, c) for s in range(LEVELS) for i in range(-1, s) for c in range(PARTS)]
MESH = pl.DeviceIdType.MESH
BASE2 = math.log2(math.e) / math.sqrt(HD)


def halving(rows):
    out = lax.broadcasted_iota(jnp.int32, (rows // 2, rows), 0)
    into = lax.broadcasted_iota(jnp.int32, (rows // 2, rows), 1)
    return jnp.where(into // 2 == out, 0.5, 0.0).astype(jnp.bfloat16)


def scores_of(keys, query):
    return lax.dot_general(keys, query, (((1,), (1,)), ((), ())), preferred_element_type=jnp.float32)


def weighted(values, weights):
    return lax.dot_general(
        values, weights.astype(jnp.bfloat16), (((0,), (0,)), ((), ())), preferred_element_type=jnp.float32
    )


def softened(scores):
    top = jnp.max(scores, axis=0, keepdims=True)
    weights = jnp.exp2((scores - top) * BASE2)
    return top * BASE2, weights, jnp.sum(weights, axis=0, keepdims=True)


def merged(old, new):
    joint = jnp.maximum(old[0], new[0])
    old_weight = jnp.exp2(old[0] - joint)
    new_weight = jnp.exp2(new[0] - joint)
    return (
        joint,
        old[1] * old_weight + new[1] * new_weight,
        old[2] * old_weight + new[2] * new_weight,
    )


def kernel(head_bits, q_ref, k_ref, v_ref, o_ref, *scratch):
    pyramid = scratch[:LEVELS]
    tiles = scratch[LEVELS : 2 * LEVELS]
    numerators, tops, denominators, send_sems, recv_sems = scratch[2 * LEVELS :]
    width = q_ref.shape[1]
    heads = width // HD
    seq, head = lax.axis_index("seq"), lax.axis_index("head")

    def bit(b):
        return head // 2**b % 2 if b < head_bits else seq // 2 ** (b - head_bits) % 2

    def partner(b):
        step = 1 - 2 * bit(b)
        if b < head_bits:
            return (seq, head + step * 2**b)
        return (seq + step * 2 ** (b - head_bits), head)

    def slot(s):
        where = 0
        for i, b in enumerate(ORDER[s]):
            where = where + bit(b) * 2**i
        return where

    def copy(s, i, c):
        n = COPIES.index((s, i, c))
        part = pl.ds(c * (width // PARTS), width // PARTS)
        if i < 0:
            source, target, b = pyramid[s].at[:, part], tiles[s].at[slot(s), :, part], s
        else:
            block = pl.ds(slot(s) // 2**i * 2**i, 2**i)
            source = target = tiles[s].at[block, :, part]
            b = ORDER[s][i]
        return pltpu.make_async_remote_copy(
            src_ref=source, dst_ref=target, send_sem=send_sems.at[n], recv_sem=recv_sems.at[n],
            device_id=partner(b), device_id_type=MESH,
        )

    def landed(s, i, c):
        @pl.when(bit(s) == 1)
        def _():
            copy(s, i, c).wait_recv()
            if i + 1 < s:
                copy(s, i + 1, c).start()

    def push(s, c):
        @pl.when(bit(s) == 0)
        def _():
            copy(s, -1, c).start()

    barrier = pltpu.get_barrier_semaphore()
    for b in range(LEVELS):
        pl.semaphore_signal(barrier, inc=1, device_id=partner(b), device_id_type=MESH)

    chunk = 512

    def coarsen(part):
        @pl.loop(part * (width // chunk // PARTS), (part + 1) * (width // chunk // PARTS))
        def _(c):
            columns = pl.ds(pl.multiple_of(c * chunk, chunk), chunk)
            keys, values = k_ref[:, columns], v_ref[:, columns]
            for s in range(LEVELS):
                rows = BLOCK // 2**s
                mean = halving(2 * rows)
                keys = jnp.dot(mean, keys, preferred_element_type=jnp.float32)
                values = jnp.dot(mean, values, preferred_element_type=jnp.float32)
                pyramid[s][:, columns] = jnp.concatenate([keys, values], axis=0).astype(jnp.bfloat16)
                keys, values = keys.astype(jnp.bfloat16), values.astype(jnp.bfloat16)

    def columns_of(h):
        return pl.ds(pl.multiple_of(h * HD, HD), HD)

    def store(group, states):
        for h, state in zip(group, states):
            tops[h] = state[0]
            numerators[h] = state[1]
            denominators[h] = state[2]

    def attend(items):
        scores = [scores_of(keys, query) for keys, query, _, _ in items]
        scores = [
            s if item[3] is None else jnp.where(item[3], s, -jnp.inf) for s, item in zip(scores, items)
        ]
        soft = [softened(s) for s in scores]
        sums = [weighted(item[2], weights) for item, (_, weights, _) in zip(items, soft)]
        return [(top, n, total) for (top, _, total), n in zip(soft, sums)]

    def local(group):
        key = lax.broadcasted_iota(jnp.int32, (BLOCK, BLOCK), 0)
        token = lax.broadcasted_iota(jnp.int32, (BLOCK, BLOCK), 1)
        causal = key <= token
        items = []
        for h in group:
            columns = columns_of(h)
            query = [q_ref[pl.ds(r * BLOCK, BLOCK), columns] for r in range(2)]
            keys = [k_ref[pl.ds(r * BLOCK, BLOCK), columns] for r in range(2)]
            values = [v_ref[pl.ds(r * BLOCK, BLOCK), columns] for r in range(2)]
            items += [
                (keys[0], query[0], values[0], causal),
                (keys[1], query[1], values[1], causal),
                (keys[0], query[1], values[0], None),
            ]
        levels = attend(items)
        states = []
        for u in range(len(group)):
            first, second = levels[3 * u], merged(levels[3 * u + 1], levels[3 * u + 2])
            states.append([jnp.concatenate(two, axis=1) for two in zip(first, second)])
        store(group, states)

    def far(s, c):
        rows = BLOCK // 2**s

        def of_group(group):
            items = []
            for h in group:
                columns = columns_of(h)
                if rows >= 16:
                    keys = tiles[s][:, :rows, columns].reshape(BLOCK, HD)
                    values = tiles[s][:, rows:, columns].reshape(BLOCK, HD)
                else:
                    both = tiles[s][:, :, columns].astype(jnp.float32)
                    keys = both[:, :rows].reshape(BLOCK, HD).astype(jnp.bfloat16)
                    values = both[:, rows:].reshape(BLOCK, HD).astype(jnp.bfloat16)
                items.append((keys, q_ref[:, columns], values, None))
            olds = [(tops[h], numerators[h], denominators[h]) for h in group]
            levels = [(top + (s + 1.0), n, total) for top, n, total in attend(items)]
            store(group, [merged(old, level) for old, level in zip(olds, levels)])

        @pl.when(bit(s) == 1)
        def _():
            each(of_group, c)

    def each(of_group, c):
        count = heads // PARTS // UNROLL

        @pl.loop(c * count, (c + 1) * count)
        def _(g):
            of_group([g * UNROLL + u for u in range(UNROLL)])

    def final(group):
        results = [(numerators[h] * (1.0 / denominators[h])).T.astype(o_ref.dtype) for h in group]
        for h, result in zip(group, results):
            o_ref[:, columns_of(h)] = result

    coarsen(0)
    pl.semaphore_wait(barrier, LEVELS)
    for s in (4, 3, 2, 1, 0):
        push(s, 0)
    coarsen(1)
    for s in (4, 3, 2, 0):
        push(s, 1)
    each(local, 0)
    for c in range(PARTS):
        landed(3, -1, c)
        landed(4, -1, c)
    each(local, 1)
    landed(2, -1, 0)
    landed(2, -1, 1)
    push(1, 1)
    landed(0, -1, 0)
    far(0, 0)
    landed(3, 0, 0)
    landed(4, 0, 0)
    landed(0, -1, 1)
    far(0, 1)
    landed(3, 0, 1)
    landed(4, 0, 1)
    landed(1, -1, 0)
    landed(4, 1, 0)
    landed(4, 1, 1)
    landed(1, 0, 0)
    far(1, 0)
    landed(3, 1, 0)
    landed(2, 0, 0)
    landed(3, 1, 1)
    landed(4, 2, 0)
    landed(3, 2, 0)
    far(3, 0)
    landed(2, 1, 0)
    far(2, 0)
    landed(4, 2, 1)
    landed(2, 0, 1)
    landed(3, 2, 1)
    far(3, 1)
    landed(4, 3, 0)
    far(4, 0)
    each(final, 0)
    landed(4, 3, 1)
    far(4, 1)
    landed(1, -1, 1)
    landed(2, 1, 1)
    far(2, 1)
    landed(1, 0, 1)
    far(1, 1)
    each(final, 1)
    for s, i, c in COPIES:
        @pl.when(bit(s) == (0 if i < 0 else 1))
        def _():
            copy(s, i, c).wait_send()


UNROLL = 8


def fused(head_bits, queries, keys, values):
    length, width = queries.shape
    heads = width // HD
    pieces = [(2 * BLOCK // 2**s, width) for s in range(LEVELS)]
    scratch = [pltpu.VMEM(p, jnp.bfloat16) for p in pieces]
    scratch += [pltpu.VMEM((2**s,) + p, jnp.bfloat16) for s, p in enumerate(pieces)]
    scratch += [
        pltpu.VMEM((heads, HD, length), jnp.float32),
        pltpu.VMEM((heads, 1, length), jnp.float32),
        pltpu.VMEM((heads, 1, length), jnp.float32),
        pltpu.SemaphoreType.DMA((len(COPIES),)),
        pltpu.SemaphoreType.DMA((len(COPIES),)),
    ]
    return pl.pallas_call(
        functools.partial(kernel, head_bits),
        out_shape=jax.ShapeDtypeStruct((length, width), jnp.bfloat16),
        in_specs=[pl.BlockSpec(memory_space=pltpu.VMEM)] * 3,
        out_specs=pl.BlockSpec(memory_space=pltpu.VMEM),
        scratch_shapes=scratch,
        compiler_params=pltpu.CompilerParams(
            collective_id=0, has_side_effects=True, vmem_limit_bytes=48 * 2**20
        ),
    )(queries, keys, values)


def solution(mesh):
    if mesh.size == 2**LEVELS:
        body = functools.partial(fused, mesh.shape["head"].bit_length() - 1)
    else:
        body = shards
    return jax.shard_map(
        body,
        mesh=mesh,
        in_specs=(P(("seq", "head"), None), P(("seq", "head"), None), P(("seq", "head"), None)),
        out_specs=P(("seq", "head"), None),
        check_vma=False,
    )
```

```python
import functools
import math

import jax
import jax.numpy as jnp
from jax import lax
from jax.experimental import pallas as pl
from jax.experimental.pallas import tpu as pltpu
from jax.sharding import PartitionSpec as P

HD = 128
BLOCK = 128


def swapped(x, axis, distance):
    return lax.ppermute(x, axis, [(i, i ^ 1 << distance) for i in range(lax.axis_size(axis))])


def halve(field):
    rows = field.shape[0]
    paired = field.astype(jnp.float32).reshape((rows // 2, 2) + field.shape[1:])
    return ((paired[:, 0] + paired[:, 1]) * 0.5).astype(jnp.bfloat16)


def merge_level(state, level):
    best, numerator, denominator = state
    level_top, level_numerator, level_denominator = level
    joint = jnp.maximum(best, level_top)
    old_weight = jnp.exp(best - joint)
    new_weight = jnp.exp(level_top - joint)
    return (
        joint,
        numerator * old_weight[:, :, None] + level_numerator * new_weight[:, :, None],
        denominator * old_weight + level_denominator * new_weight,
    )


def leaf_level(query, keys_local, values_local, scale):
    length, heads, width = query.shape
    blocks = length // BLOCK
    shaped = (blocks, BLOCK, heads, width)
    scores = (
        jnp.einsum(
            "nigd,njgd->ngij",
            query.reshape(shaped),
            keys_local.reshape(shaped),
            preferred_element_type=jnp.float32,
        )
        * scale
    )
    causal = jnp.arange(BLOCK)[:, None] >= jnp.arange(BLOCK)[None, :]
    top = jnp.max(jnp.where(causal, scores, -jnp.inf), axis=-1)
    weights = jnp.where(causal, jnp.exp(scores - top[..., None]), 0.0)
    numerator = jnp.einsum(
        "ngij,njgd->nigd",
        weights.astype(jnp.bfloat16),
        values_local.reshape(shaped),
        preferred_element_type=jnp.float32,
    )
    denominator = jnp.sum(weights, axis=-1)
    top = top.transpose(0, 2, 1).reshape(length, heads)
    denominator = denominator.transpose(0, 2, 1).reshape(length, heads)
    return (top, numerator.reshape(length, heads, width), denominator)


def pair_level(query, coarse_keys, coarse_values, level, scale):
    length, heads, width = query.shape
    span = BLOCK * 2 ** (level - 1)
    pairs = length // (2 * span)
    upper_queries = query.reshape(pairs, 2, span, heads, width)[:, 1]
    lower_keys = coarse_keys.reshape(pairs, 2, BLOCK, heads, width)[:, 0]
    lower_values = coarse_values.reshape(pairs, 2, BLOCK, heads, width)[:, 0]
    scores = jnp.einsum(
        "npgd,nbgd->npgb", upper_queries, lower_keys, preferred_element_type=jnp.float32
    ) * scale + (level - 1) * math.log(2.0)
    top = jnp.max(scores, axis=-1)
    weights = jnp.exp(scores - top[..., None])
    numerator = jnp.einsum(
        "npgb,nbgd->npgd",
        weights.astype(jnp.bfloat16),
        lower_values,
        preferred_element_type=jnp.float32,
    )
    denominator = jnp.sum(weights, axis=-1)
    top_full = jnp.stack([jnp.full_like(top, -jnp.inf), top], axis=1).reshape(length, heads)
    numerator_full = jnp.stack([jnp.zeros_like(numerator), numerator], axis=1).reshape(
        length, heads, width
    )
    denominator_full = jnp.stack([jnp.zeros_like(denominator), denominator], axis=1).reshape(
        length, heads
    )
    return (top_full, numerator_full, denominator_full)


def far_level(query, tile_keys, tile_values, level, scale, upper):
    length, heads, width = query.shape

    def active():
        scores = jnp.einsum(
            "sgd,bgd->sgb", query, tile_keys, preferred_element_type=jnp.float32
        ) * scale + (level - 1) * math.log(2.0)
        top = jnp.max(scores, axis=-1)
        weights = jnp.exp(scores - top[..., None])
        numerator = jnp.einsum(
            "sgb,bgd->sgd",
            weights.astype(jnp.bfloat16),
            tile_values,
            preferred_element_type=jnp.float32,
        )
        return (top, numerator, jnp.sum(weights, axis=-1))

    def quiet():
        return (
            jnp.full((length, heads), -jnp.inf, jnp.float32),
            jnp.zeros((length, heads, width), jnp.float32),
            jnp.zeros((length, heads), jnp.float32),
        )

    return lax.cond(upper == 1, active, quiet)


def local_part(query, keys_local, values_local, scale):
    state = leaf_level(query, keys_local, values_local, scale)
    depth = (query.shape[0] // BLOCK).bit_length() - 1
    coarse_keys, coarse_values = (keys_local, values_local)
    state = merge_level(state, pair_level(query, coarse_keys, coarse_values, 1, scale))
    coarse_keys = halve(coarse_keys)
    coarse_values = halve(coarse_values)
    return (state, coarse_keys, coarse_values, depth + 1)


def doubling(query, state, tile_keys, tile_values, first, count, position, trade, scale):
    for step in range(count):
        other_keys, other_values = trade(tile_keys, tile_values, step)
        upper = position // 2**step % 2
        state = merge_level(
            state, far_level(query, other_keys, other_values, first + step, scale, upper)
        )
        if step + 1 < count:
            high = upper == 1
            low_keys = jnp.where(high, other_keys, tile_keys)
            high_keys = jnp.where(high, tile_keys, other_keys)
            low_values = jnp.where(high, other_values, tile_values)
            high_values = jnp.where(high, tile_values, other_values)
            tile_keys = halve(jnp.concatenate([low_keys, high_keys], axis=0))
            tile_values = halve(jnp.concatenate([low_values, high_values], axis=0))
    return state


def finish(state):
    best, numerator, denominator = state
    length, heads, width = numerator.shape
    return (numerator / denominator[:, :, None]).astype(jnp.bfloat16).reshape(length, heads * width)


def shards(queries, keys, values):
    scale = 1.0 / math.sqrt(HD)
    length, width = queries.shape
    cube_shape = (length, width // HD, HD)
    query = queries.reshape(cube_shape)
    state, tile_keys, tile_values, first = local_part(
        query, keys.reshape(cube_shape), values.reshape(cube_shape), scale
    )
    position = lax.axis_index(("seq", "head"))
    count = lax.axis_size(("seq", "head")).bit_length() - 1

    def trade_all(send_keys, send_values, bit):
        return swapped((send_keys, send_values), ("seq", "head"), bit)

    state = doubling(query, state, tile_keys, tile_values, first, count, position, trade_all, scale)
    return finish(state)


LEVELS = 5
ORDER = {0: (), 1: (0,), 2: (1, 0), 3: (1, 2, 0), 4: (1, 2, 3, 0)}
PARTS = 2
COPIES = [(s, i, c) for s in range(LEVELS) for i in range(-1, s) for c in range(PARTS)]
MESH = pl.DeviceIdType.MESH
BASE2 = math.log2(math.e) / math.sqrt(HD)


def halving(rows):
    out = lax.broadcasted_iota(jnp.int32, (rows // 2, rows), 0)
    into = lax.broadcasted_iota(jnp.int32, (rows // 2, rows), 1)
    return jnp.where(into // 2 == out, 0.5, 0.0).astype(jnp.bfloat16)


def scores_of(keys, query):
    return lax.dot_general(keys, query, (((1,), (1,)), ((), ())), preferred_element_type=jnp.float32)


def weighted(values, weights):
    return lax.dot_general(
        values, weights.astype(jnp.bfloat16), (((0,), (0,)), ((), ())), preferred_element_type=jnp.float32
    )


def softened(scores):
    top = jnp.max(scores, axis=0, keepdims=True)
    weights = jnp.exp2((scores - top) * BASE2)
    return top * BASE2, weights, jnp.sum(weights, axis=0, keepdims=True)


def merged(old, new):
    joint = jnp.maximum(old[0], new[0])
    old_weight = jnp.exp2(old[0] - joint)
    new_weight = jnp.exp2(new[0] - joint)
    return (
        joint,
        old[1] * old_weight + new[1] * new_weight,
        old[2] * old_weight + new[2] * new_weight,
    )


def kernel(head_bits, q_ref, k_ref, v_ref, o_ref, *scratch):
    pyramid = scratch[:LEVELS]
    tiles = scratch[LEVELS : 2 * LEVELS]
    numerators, tops, denominators, send_sems, recv_sems = scratch[2 * LEVELS :]
    width = q_ref.shape[1]
    heads = width // HD
    seq, head = lax.axis_index("seq"), lax.axis_index("head")

    def bit(b):
        return head // 2**b % 2 if b < head_bits else seq // 2 ** (b - head_bits) % 2

    def partner(b):
        step = 1 - 2 * bit(b)
        if b < head_bits:
            return (seq, head + step * 2**b)
        return (seq + step * 2 ** (b - head_bits), head)

    def slot(s):
        where = 0
        for i, b in enumerate(ORDER[s]):
            where = where + bit(b) * 2**i
        return where

    def copy(s, i, c):
        n = COPIES.index((s, i, c))
        part = pl.ds(c * (width // PARTS), width // PARTS)
        if i < 0:
            source, target, b = pyramid[s].at[:, part], tiles[s].at[slot(s), :, part], s
        else:
            block = pl.ds(slot(s) // 2**i * 2**i, 2**i)
            source = target = tiles[s].at[block, :, part]
            b = ORDER[s][i]
        return pltpu.make_async_remote_copy(
            src_ref=source, dst_ref=target, send_sem=send_sems.at[n], recv_sem=recv_sems.at[n],
            device_id=partner(b), device_id_type=MESH,
        )

    def landed(s, i, c):
        @pl.when(bit(s) == 1)
        def _():
            copy(s, i, c).wait_recv()
            if i + 1 < s:
                copy(s, i + 1, c).start()

    def push(s, c):
        @pl.when(bit(s) == 0)
        def _():
            copy(s, -1, c).start()

    barrier = pltpu.get_barrier_semaphore()
    for b in range(LEVELS):
        pl.semaphore_signal(barrier, inc=1, device_id=partner(b), device_id_type=MESH)

    chunk = 512

    def coarsen(part):
        @pl.loop(part * (width // chunk // PARTS), (part + 1) * (width // chunk // PARTS))
        def _(c):
            columns = pl.ds(pl.multiple_of(c * chunk, chunk), chunk)
            keys, values = k_ref[:, columns], v_ref[:, columns]
            for s in range(LEVELS):
                rows = BLOCK // 2**s
                mean = halving(2 * rows)
                keys = jnp.dot(mean, keys, preferred_element_type=jnp.float32)
                values = jnp.dot(mean, values, preferred_element_type=jnp.float32)
                pyramid[s][:, columns] = jnp.concatenate([keys, values], axis=0).astype(jnp.bfloat16)
                keys, values = keys.astype(jnp.bfloat16), values.astype(jnp.bfloat16)

    def columns_of(h):
        return pl.ds(pl.multiple_of(h * HD, HD), HD)

    def store(group, states):
        for h, state in zip(group, states):
            tops[h] = state[0]
            numerators[h] = state[1]
            denominators[h] = state[2]

    def attend(items):
        scores = [scores_of(keys, query) for keys, query, _, _ in items]
        scores = [
            s if item[3] is None else jnp.where(item[3], s, -jnp.inf) for s, item in zip(scores, items)
        ]
        soft = [softened(s) for s in scores]
        sums = [weighted(item[2], weights) for item, (_, weights, _) in zip(items, soft)]
        return [(top, n, total) for (top, _, total), n in zip(soft, sums)]

    def local(group):
        key = lax.broadcasted_iota(jnp.int32, (BLOCK, BLOCK), 0)
        token = lax.broadcasted_iota(jnp.int32, (BLOCK, BLOCK), 1)
        causal = key <= token
        items = []
        for h in group:
            columns = columns_of(h)
            query = [q_ref[pl.ds(r * BLOCK, BLOCK), columns] for r in range(2)]
            keys = [k_ref[pl.ds(r * BLOCK, BLOCK), columns] for r in range(2)]
            values = [v_ref[pl.ds(r * BLOCK, BLOCK), columns] for r in range(2)]
            items += [
                (keys[0], query[0], values[0], causal),
                (keys[1], query[1], values[1], causal),
                (keys[0], query[1], values[0], None),
            ]
        levels = attend(items)
        states = []
        for u in range(len(group)):
            first, second = levels[3 * u], merged(levels[3 * u + 1], levels[3 * u + 2])
            states.append([jnp.concatenate(two, axis=1) for two in zip(first, second)])
        store(group, states)

    def far(s, c):
        rows = BLOCK // 2**s

        def of_group(group):
            items = []
            for h in group:
                columns = columns_of(h)
                if rows >= 16:
                    keys = tiles[s][:, :rows, columns].reshape(BLOCK, HD)
                    values = tiles[s][:, rows:, columns].reshape(BLOCK, HD)
                else:
                    both = tiles[s][:, :, columns].astype(jnp.float32)
                    keys = both[:, :rows].reshape(BLOCK, HD).astype(jnp.bfloat16)
                    values = both[:, rows:].reshape(BLOCK, HD).astype(jnp.bfloat16)
                items.append((keys, q_ref[:, columns], values, None))
            olds = [(tops[h], numerators[h], denominators[h]) for h in group]
            levels = [(top + (s + 1.0), n, total) for top, n, total in attend(items)]
            store(group, [merged(old, level) for old, level in zip(olds, levels)])

        @pl.when(bit(s) == 1)
        def _():
            each(of_group, c)

    def each(of_group, c):
        count = heads // PARTS // UNROLL

        @pl.loop(c * count, (c + 1) * count)
        def _(g):
            of_group([g * UNROLL + u for u in range(UNROLL)])

    def final(group):
        results = [(numerators[h] * (1.0 / denominators[h])).T.astype(o_ref.dtype) for h in group]
        for h, result in zip(group, results):
            o_ref[:, columns_of(h)] = result

    coarsen(0)
    pl.semaphore_wait(barrier, LEVELS)
    for s in (4, 3, 2, 1, 0):
        push(s, 0)
    coarsen(1)
    for s in (4, 3, 2, 0):
        push(s, 1)
    each(local, 0)
    for c in range(PARTS):
        landed(3, -1, c)
        landed(4, -1, c)
    each(local, 1)
    landed(2, -1, 0)
    landed(2, -1, 1)
    push(1, 1)
    landed(0, -1, 0)
    far(0, 0)
    landed(3, 0, 0)
    landed(4, 0, 0)
    landed(0, -1, 1)
    far(0, 1)
    landed(3, 0, 1)
    landed(4, 0, 1)
    landed(1, -1, 0)
    landed(4, 1, 0)
    landed(4, 1, 1)
    landed(1, 0, 0)
    far(1, 0)
    landed(3, 1, 0)
    landed(2, 0, 0)
    landed(3, 1, 1)
    landed(4, 2, 0)
    landed(3, 2, 0)
    far(3, 0)
    landed(2, 1, 0)
    far(2, 0)
    landed(4, 2, 1)
    landed(2, 0, 1)
    landed(3, 2, 1)
    far(3, 1)
    landed(4, 3, 0)
    far(4, 0)
    landed(1, -1, 1)
    each(final, 0)
    landed(4, 3, 1)
    far(4, 1)
    landed(2, 1, 1)
    far(2, 1)
    landed(1, 0, 1)
    far(1, 1)
    each(final, 1)
    for s, i, c in COPIES:
        @pl.when(bit(s) == (0 if i < 0 else 1))
        def _():
            copy(s, i, c).wait_send()


UNROLL = 8


def fused(head_bits, queries, keys, values):
    length, width = queries.shape
    heads = width // HD
    pieces = [(2 * BLOCK // 2**s, width) for s in range(LEVELS)]
    scratch = [pltpu.VMEM(p, jnp.bfloat16) for p in pieces]
    scratch += [pltpu.VMEM((2**s,) + p, jnp.bfloat16) for s, p in enumerate(pieces)]
    scratch += [
        pltpu.VMEM((heads, HD, length), jnp.float32),
        pltpu.VMEM((heads, 1, length), jnp.float32),
        pltpu.VMEM((heads, 1, length), jnp.float32),
        pltpu.SemaphoreType.DMA((len(COPIES),)),
        pltpu.SemaphoreType.DMA((len(COPIES),)),
    ]
    return pl.pallas_call(
        functools.partial(kernel, head_bits),
        out_shape=jax.ShapeDtypeStruct((length, width), jnp.bfloat16),
        in_specs=[pl.BlockSpec(memory_space=pltpu.VMEM)] * 3,
        out_specs=pl.BlockSpec(memory_space=pltpu.VMEM),
        scratch_shapes=scratch,
        compiler_params=pltpu.CompilerParams(
            collective_id=0, has_side_effects=True, vmem_limit_bytes=48 * 2**20
        ),
    )(queries, keys, values)


def solution(mesh):
    if mesh.size == 2**LEVELS:
        body = functools.partial(fused, mesh.shape["head"].bit_length() - 1)
    else:
        body = shards
    return jax.shard_map(
        body,
        mesh=mesh,
        in_specs=(P(("seq", "head"), None), P(("seq", "head"), None), P(("seq", "head"), None)),
        out_specs=P(("seq", "head"), None),
        check_vma=False,
    )
```

```python
import functools
import math

import jax
import jax.numpy as jnp
from jax import lax
from jax.experimental import pallas as pl
from jax.experimental.pallas import tpu as pltpu
from jax.sharding import PartitionSpec as P

HD = 128
BLOCK = 128


def swapped(x, axis, distance):
    return lax.ppermute(x, axis, [(i, i ^ 1 << distance) for i in range(lax.axis_size(axis))])


def halve(field):
    rows = field.shape[0]
    paired = field.astype(jnp.float32).reshape((rows // 2, 2) + field.shape[1:])
    return ((paired[:, 0] + paired[:, 1]) * 0.5).astype(jnp.bfloat16)


def merge_level(state, level):
    best, numerator, denominator = state
    level_top, level_numerator, level_denominator = level
    joint = jnp.maximum(best, level_top)
    old_weight = jnp.exp(best - joint)
    new_weight = jnp.exp(level_top - joint)
    return (
        joint,
        numerator * old_weight[:, :, None] + level_numerator * new_weight[:, :, None],
        denominator * old_weight + level_denominator * new_weight,
    )


def leaf_level(query, keys_local, values_local, scale):
    length, heads, width = query.shape
    blocks = length // BLOCK
    shaped = (blocks, BLOCK, heads, width)
    scores = (
        jnp.einsum(
            "nigd,njgd->ngij",
            query.reshape(shaped),
            keys_local.reshape(shaped),
            preferred_element_type=jnp.float32,
        )
        * scale
    )
    causal = jnp.arange(BLOCK)[:, None] >= jnp.arange(BLOCK)[None, :]
    top = jnp.max(jnp.where(causal, scores, -jnp.inf), axis=-1)
    weights = jnp.where(causal, jnp.exp(scores - top[..., None]), 0.0)
    numerator = jnp.einsum(
        "ngij,njgd->nigd",
        weights.astype(jnp.bfloat16),
        values_local.reshape(shaped),
        preferred_element_type=jnp.float32,
    )
    denominator = jnp.sum(weights, axis=-1)
    top = top.transpose(0, 2, 1).reshape(length, heads)
    denominator = denominator.transpose(0, 2, 1).reshape(length, heads)
    return (top, numerator.reshape(length, heads, width), denominator)


def pair_level(query, coarse_keys, coarse_values, level, scale):
    length, heads, width = query.shape
    span = BLOCK * 2 ** (level - 1)
    pairs = length // (2 * span)
    upper_queries = query.reshape(pairs, 2, span, heads, width)[:, 1]
    lower_keys = coarse_keys.reshape(pairs, 2, BLOCK, heads, width)[:, 0]
    lower_values = coarse_values.reshape(pairs, 2, BLOCK, heads, width)[:, 0]
    scores = jnp.einsum(
        "npgd,nbgd->npgb", upper_queries, lower_keys, preferred_element_type=jnp.float32
    ) * scale + (level - 1) * math.log(2.0)
    top = jnp.max(scores, axis=-1)
    weights = jnp.exp(scores - top[..., None])
    numerator = jnp.einsum(
        "npgb,nbgd->npgd",
        weights.astype(jnp.bfloat16),
        lower_values,
        preferred_element_type=jnp.float32,
    )
    denominator = jnp.sum(weights, axis=-1)
    top_full = jnp.stack([jnp.full_like(top, -jnp.inf), top], axis=1).reshape(length, heads)
    numerator_full = jnp.stack([jnp.zeros_like(numerator), numerator], axis=1).reshape(
        length, heads, width
    )
    denominator_full = jnp.stack([jnp.zeros_like(denominator), denominator], axis=1).reshape(
        length, heads
    )
    return (top_full, numerator_full, denominator_full)


def far_level(query, tile_keys, tile_values, level, scale, upper):
    length, heads, width = query.shape

    def active():
        scores = jnp.einsum(
            "sgd,bgd->sgb", query, tile_keys, preferred_element_type=jnp.float32
        ) * scale + (level - 1) * math.log(2.0)
        top = jnp.max(scores, axis=-1)
        weights = jnp.exp(scores - top[..., None])
        numerator = jnp.einsum(
            "sgb,bgd->sgd",
            weights.astype(jnp.bfloat16),
            tile_values,
            preferred_element_type=jnp.float32,
        )
        return (top, numerator, jnp.sum(weights, axis=-1))

    def quiet():
        return (
            jnp.full((length, heads), -jnp.inf, jnp.float32),
            jnp.zeros((length, heads, width), jnp.float32),
            jnp.zeros((length, heads), jnp.float32),
        )

    return lax.cond(upper == 1, active, quiet)


def local_part(query, keys_local, values_local, scale):
    state = leaf_level(query, keys_local, values_local, scale)
    depth = (query.shape[0] // BLOCK).bit_length() - 1
    coarse_keys, coarse_values = (keys_local, values_local)
    state = merge_level(state, pair_level(query, coarse_keys, coarse_values, 1, scale))
    coarse_keys = halve(coarse_keys)
    coarse_values = halve(coarse_values)
    return (state, coarse_keys, coarse_values, depth + 1)


def doubling(query, state, tile_keys, tile_values, first, count, position, trade, scale):
    for step in range(count):
        other_keys, other_values = trade(tile_keys, tile_values, step)
        upper = position // 2**step % 2
        state = merge_level(
            state, far_level(query, other_keys, other_values, first + step, scale, upper)
        )
        if step + 1 < count:
            high = upper == 1
            low_keys = jnp.where(high, other_keys, tile_keys)
            high_keys = jnp.where(high, tile_keys, other_keys)
            low_values = jnp.where(high, other_values, tile_values)
            high_values = jnp.where(high, tile_values, other_values)
            tile_keys = halve(jnp.concatenate([low_keys, high_keys], axis=0))
            tile_values = halve(jnp.concatenate([low_values, high_values], axis=0))
    return state


def finish(state):
    best, numerator, denominator = state
    length, heads, width = numerator.shape
    return (numerator / denominator[:, :, None]).astype(jnp.bfloat16).reshape(length, heads * width)


def shards(queries, keys, values):
    scale = 1.0 / math.sqrt(HD)
    length, width = queries.shape
    cube_shape = (length, width // HD, HD)
    query = queries.reshape(cube_shape)
    state, tile_keys, tile_values, first = local_part(
        query, keys.reshape(cube_shape), values.reshape(cube_shape), scale
    )
    position = lax.axis_index(("seq", "head"))
    count = lax.axis_size(("seq", "head")).bit_length() - 1

    def trade_all(send_keys, send_values, bit):
        return swapped((send_keys, send_values), ("seq", "head"), bit)

    state = doubling(query, state, tile_keys, tile_values, first, count, position, trade_all, scale)
    return finish(state)


LEVELS = 5
ORDER = {0: (), 1: (0,), 2: (1, 0), 3: (1, 2, 0), 4: (1, 2, 3, 0)}
PARTS = 2
COPIES = [(s, i, c) for s in range(LEVELS) for i in range(-1, s) for c in range(PARTS)]
MESH = pl.DeviceIdType.MESH
BASE2 = math.log2(math.e) / math.sqrt(HD)


def halving(rows):
    out = lax.broadcasted_iota(jnp.int32, (rows // 2, rows), 0)
    into = lax.broadcasted_iota(jnp.int32, (rows // 2, rows), 1)
    return jnp.where(into // 2 == out, 0.5, 0.0).astype(jnp.bfloat16)


def scores_of(keys, query):
    return lax.dot_general(keys, query, (((1,), (1,)), ((), ())), preferred_element_type=jnp.float32)


def weighted(values, weights):
    return lax.dot_general(
        values, weights.astype(jnp.bfloat16), (((0,), (0,)), ((), ())), preferred_element_type=jnp.float32
    )


def softened(scores):
    top = jnp.max(scores, axis=0, keepdims=True)
    weights = jnp.exp2((scores - top) * BASE2)
    return top * BASE2, weights, jnp.sum(weights, axis=0, keepdims=True)


def merged(old, new):
    joint = jnp.maximum(old[0], new[0])
    old_weight = jnp.exp2(old[0] - joint)
    new_weight = jnp.exp2(new[0] - joint)
    return (
        joint,
        old[1] * old_weight + new[1] * new_weight,
        old[2] * old_weight + new[2] * new_weight,
    )


def kernel(head_bits, q_ref, k_ref, v_ref, o_ref, *scratch):
    pyramid = scratch[:LEVELS]
    tiles = scratch[LEVELS : 2 * LEVELS]
    numerators, tops, denominators, send_sems, recv_sems = scratch[2 * LEVELS :]
    width = q_ref.shape[1]
    heads = width // HD
    seq, head = lax.axis_index("seq"), lax.axis_index("head")

    def bit(b):
        return head // 2**b % 2 if b < head_bits else seq // 2 ** (b - head_bits) % 2

    def partner(b):
        step = 1 - 2 * bit(b)
        if b < head_bits:
            return (seq, head + step * 2**b)
        return (seq + step * 2 ** (b - head_bits), head)

    def slot(s):
        where = 0
        for i, b in enumerate(ORDER[s]):
            where = where + bit(b) * 2**i
        return where

    def copy(s, i, c):
        n = COPIES.index((s, i, c))
        part = pl.ds(c * (width // PARTS), width // PARTS)
        if i < 0:
            source, target, b = pyramid[s].at[:, part], tiles[s].at[slot(s), :, part], s
        else:
            block = pl.ds(slot(s) // 2**i * 2**i, 2**i)
            source = target = tiles[s].at[block, :, part]
            b = ORDER[s][i]
        return pltpu.make_async_remote_copy(
            src_ref=source, dst_ref=target, send_sem=send_sems.at[n], recv_sem=recv_sems.at[n],
            device_id=partner(b), device_id_type=MESH,
        )

    def relayed():
        part = pl.ds(0, width // PARTS)
        return pltpu.make_async_remote_copy(
            src_ref=tiles[2].at[slot(2) - 1, :, part], dst_ref=tiles[2].at[slot(2) - 1, :, part],
            send_sem=send_sems.at[COPIES.index((2, 0, 0))], recv_sem=recv_sems.at[COPIES.index((2, 0, 0))],
            device_id=partner(2), device_id_type=MESH,
        )

    def relay():
        @pl.when((1 - bit(2)) * bit(1) == 1)
        def _():
            @pl.loop(0, width // chunk // PARTS)
            def _(c):
                columns = pl.ds(pl.multiple_of(c * chunk, chunk), chunk)
                mean = halving(64)
                held = tiles[1].at[slot(1)]
                keys = jnp.dot(mean, held[:64, columns], preferred_element_type=jnp.float32)
                values = jnp.dot(mean, held[64:, columns], preferred_element_type=jnp.float32)
                tiles[2][slot(2) - 1, :, columns] = jnp.concatenate([keys, values], axis=0).astype(jnp.bfloat16)

            relayed().start()

    def landed(s, i, c):
        @pl.when(bit(s) == 1)
        def _():
            copy(s, i, c).wait_recv()
            if (s, i, c) == (2, -1, 0):
                @pl.when(bit(1) == 1)
                def _():
                    copy(2, 0, 0).start()
            elif i + 1 < s:
                copy(s, i + 1, c).start()

    def push(s, c):
        @pl.when(bit(s) == 0)
        def _():
            copy(s, -1, c).start()

    barrier = pltpu.get_barrier_semaphore()
    for b in range(LEVELS):
        pl.semaphore_signal(barrier, inc=1, device_id=partner(b), device_id_type=MESH)

    chunk = 512

    def coarsen(part):
        @pl.loop(part * (width // chunk // PARTS), (part + 1) * (width // chunk // PARTS))
        def _(c):
            columns = pl.ds(pl.multiple_of(c * chunk, chunk), chunk)
            keys, values = k_ref[:, columns], v_ref[:, columns]
            for s in range(LEVELS):
                rows = BLOCK // 2**s
                mean = halving(2 * rows)
                keys = jnp.dot(mean, keys, preferred_element_type=jnp.float32)
                values = jnp.dot(mean, values, preferred_element_type=jnp.float32)
                pyramid[s][:, columns] = jnp.concatenate([keys, values], axis=0).astype(jnp.bfloat16)
                keys, values = keys.astype(jnp.bfloat16), values.astype(jnp.bfloat16)

    def columns_of(h):
        return pl.ds(pl.multiple_of(h * HD, HD), HD)

    def store(group, states):
        for h, state in zip(group, states):
            tops[h] = state[0]
            numerators[h] = state[1]
            denominators[h] = state[2]

    def attend(items):
        scores = [scores_of(keys, query) for keys, query, _, _ in items]
        scores = [
            s if item[3] is None else jnp.where(item[3], s, -jnp.inf) for s, item in zip(scores, items)
        ]
        soft = [softened(s) for s in scores]
        sums = [weighted(item[2], weights) for item, (_, weights, _) in zip(items, soft)]
        return [(top, n, total) for (top, _, total), n in zip(soft, sums)]

    def local(group):
        key = lax.broadcasted_iota(jnp.int32, (BLOCK, BLOCK), 0)
        token = lax.broadcasted_iota(jnp.int32, (BLOCK, BLOCK), 1)
        causal = key <= token
        items = []
        for h in group:
            columns = columns_of(h)
            query = [q_ref[pl.ds(r * BLOCK, BLOCK), columns] for r in range(2)]
            keys = [k_ref[pl.ds(r * BLOCK, BLOCK), columns] for r in range(2)]
            values = [v_ref[pl.ds(r * BLOCK, BLOCK), columns] for r in range(2)]
            items += [
                (keys[0], query[0], values[0], causal),
                (keys[1], query[1], values[1], causal),
                (keys[0], query[1], values[0], None),
            ]
        levels = attend(items)
        states = []
        for u in range(len(group)):
            first, second = levels[3 * u], merged(levels[3 * u + 1], levels[3 * u + 2])
            states.append([jnp.concatenate(two, axis=1) for two in zip(first, second)])
        store(group, states)

    def far(s, c):
        rows = BLOCK // 2**s

        def of_group(group):
            items = []
            for h in group:
                columns = columns_of(h)
                if rows >= 16:
                    keys = tiles[s][:, :rows, columns].reshape(BLOCK, HD)
                    values = tiles[s][:, rows:, columns].reshape(BLOCK, HD)
                else:
                    both = tiles[s][:, :, columns].astype(jnp.float32)
                    keys = both[:, :rows].reshape(BLOCK, HD).astype(jnp.bfloat16)
                    values = both[:, rows:].reshape(BLOCK, HD).astype(jnp.bfloat16)
                items.append((keys, q_ref[:, columns], values, None))
            olds = [(tops[h], numerators[h], denominators[h]) for h in group]
            levels = [(top + (s + 1.0), n, total) for top, n, total in attend(items)]
            store(group, [merged(old, level) for old, level in zip(olds, levels)])

        @pl.when(bit(s) == 1)
        def _():
            each(of_group, c)

    def each(of_group, c):
        count = heads // PARTS // UNROLL

        @pl.loop(c * count, (c + 1) * count)
        def _(g):
            of_group([g * UNROLL + u for u in range(UNROLL)])

    def final(group):
        results = [(numerators[h] * (1.0 / denominators[h])).T.astype(o_ref.dtype) for h in group]
        for h, result in zip(group, results):
            o_ref[:, columns_of(h)] = result

    coarsen(0)
    pl.semaphore_wait(barrier, LEVELS)
    for s in (4, 3, 2, 1, 0):
        push(s, 0)
    coarsen(1)
    for s in (4, 3, 2, 0):
        push(s, 1)
    each(local, 0)
    for c in range(PARTS):
        landed(3, -1, c)
        landed(4, -1, c)
    each(local, 1)
    landed(2, -1, 0)
    landed(2, -1, 1)
    push(1, 1)
    landed(0, -1, 0)
    far(0, 0)
    landed(3, 0, 0)
    landed(4, 0, 0)
    landed(0, -1, 1)
    far(0, 1)
    landed(3, 0, 1)
    landed(4, 0, 1)
    landed(1, -1, 0)
    relay()
    landed(4, 1, 0)
    landed(4, 1, 1)
    landed(1, 0, 0)
    far(1, 0)
    landed(3, 1, 0)
    landed(2, 0, 0)
    landed(3, 1, 1)
    landed(4, 2, 0)
    landed(3, 2, 0)
    far(3, 0)
    landed(2, 1, 0)
    far(2, 0)
    landed(4, 2, 1)
    landed(2, 0, 1)
    landed(3, 2, 1)
    far(3, 1)
    landed(4, 3, 0)
    far(4, 0)
    each(final, 0)
    landed(4, 3, 1)
    far(4, 1)
    landed(1, -1, 1)
    landed(2, 1, 1)
    far(2, 1)
    landed(1, 0, 1)
    far(1, 1)
    each(final, 1)
    for s, i, c in COPIES:
        sends = bit(s) * bit(1) if (s, i, c) == (2, 0, 0) else bit(s) if i >= 0 else 1 - bit(s)

        @pl.when(sends == 1)
        def _():
            copy(s, i, c).wait_send()

    @pl.when((1 - bit(2)) * bit(1) == 1)
    def _():
        relayed().wait_send()


UNROLL = 8


def fused(head_bits, queries, keys, values):
    length, width = queries.shape
    heads = width // HD
    pieces = [(2 * BLOCK // 2**s, width) for s in range(LEVELS)]
    scratch = [pltpu.VMEM(p, jnp.bfloat16) for p in pieces]
    scratch += [pltpu.VMEM((2**s,) + p, jnp.bfloat16) for s, p in enumerate(pieces)]
    scratch += [
        pltpu.VMEM((heads, HD, length), jnp.float32),
        pltpu.VMEM((heads, 1, length), jnp.float32),
        pltpu.VMEM((heads, 1, length), jnp.float32),
        pltpu.SemaphoreType.DMA((len(COPIES),)),
        pltpu.SemaphoreType.DMA((len(COPIES),)),
    ]
    return pl.pallas_call(
        functools.partial(kernel, head_bits),
        out_shape=jax.ShapeDtypeStruct((length, width), jnp.bfloat16),
        in_specs=[pl.BlockSpec(memory_space=pltpu.VMEM)] * 3,
        out_specs=pl.BlockSpec(memory_space=pltpu.VMEM),
        scratch_shapes=scratch,
        compiler_params=pltpu.CompilerParams(
            collective_id=0, has_side_effects=True, vmem_limit_bytes=48 * 2**20
        ),
    )(queries, keys, values)


def solution(mesh):
    if mesh.size == 2**LEVELS:
        body = functools.partial(fused, mesh.shape["head"].bit_length() - 1)
    else:
        body = shards
    return jax.shard_map(
        body,
        mesh=mesh,
        in_specs=(P(("seq", "head"), None), P(("seq", "head"), None), P(("seq", "head"), None)),
        out_specs=P(("seq", "head"), None),
        check_vma=False,
    )
```
